128 devices in a mesh: gx: 8 (over y, z_lo), gy: 16 (over z_hi, x, core).
Axes of the slice: x: 4, y: 4, z: 4 (z_hi: 2, z_lo: 2; z = z_hi * 2 + z_lo), core: 2. Of those that a mesh axis runs over, the one named last changes fastest.
Arguments:
- samples: bfloat16 [512, 1024, 1024], P('gx', 'gy'), may hold values from -6 to 6
- box_labels: int32 [16], replicated, may hold values from 0 to 15, each once
Outputs:
- coefficients: float32 [8, 16, 2048, 1024], P('gx', 'gy')
The draws below stay inside these ranges and needn't reach their ends.
Inputs may be any that keep to these rules, and one draw needn't show every extreme that they name: `box_labels`: each of the 16 box labels appears exactly once.
All inputs are finite; a program needn't handle non-finite values.
Results may differ from the reference program's by a relative error of at most 0.0029.
Values sent between devices are 32-bit elements; how exact they have to be, the bound alone decides.
A program may use at most 128 MiB of HBM per device.

```python
import math
import jax
import jax.numpy as jnp
from jax import lax

N = 16384
FBY = 4
FB = 16
Q1 = 8
Q2 = 16
BX = 64
BY = 64
V = 1024
NX = 512
NY = 1024
N_GX = 8
N_GY = 16


def block_levels(key, dims, split, smallest, top_value):
    level = 1.0
    for axis_at, blocks in split:
        steps = jax.random.uniform(jax.random.fold_in(jax.random.fold_in(key, 6), axis_at), (blocks,), jnp.float32, smallest / len(split), top_value / len(split))
        level = level * jnp.repeat(jnp.exp(steps), dims[axis_at] // blocks).reshape((-1,) + (1,) * (len(dims) - 1 - axis_at))
    return level


def scatter_about(key, shape, scale, reach, pieces=(), kind=jnp.bfloat16):
    drawn = scale * jax.random.normal(key, shape, jnp.float32)
    if pieces:
        drawn = drawn * block_levels(key, shape, pieces, -0.22, 0.18)
    return jnp.clip(drawn, -reach, reach).astype(kind)


def setup_inputs(seed: int = 0) -> dict:
    key_list = jax.random.split(jax.random.key(seed), 3)
    return {
        "samples": scatter_about(key_list[0], (NX, NY, V), 1.0, 6.0, ((0, 8), (1, 16))),
        "box_labels": jax.random.permutation(key_list[1], FB).astype(jnp.int32),
    }


def cheb_nodes(points):
    counter = jnp.arange(points, dtype=jnp.float32)
    return jnp.cos(jnp.pi * (2.0 * counter + 1.0) / (2.0 * points))

def lagrange_table(cheb_points, targets):
    points = cheb_points.shape[0]
    diagonal_mask = jnp.eye(points, dtype=bool)[None, :, :]
    numerator = targets[:, None, None] - cheb_points[None, None, :]
    denominator = cheb_points[None, :, None] - cheb_points[None, None, :]
    factors = jnp.where(diagonal_mask, 1.0, numerator / jnp.where(diagonal_mask, 1.0, denominator))
    return jnp.prod(factors, axis=2)

def level_matrix(points, box_ratio, source_side, child_half):
    cheb_points = cheb_nodes(points)
    side_value = jnp.asarray(source_side).astype(jnp.float32)
    child_value = jnp.asarray(child_half).astype(jnp.float32)
    targets = child_value - 0.5 + 0.5 * cheb_points
    weights = lagrange_table(cheb_points, targets)
    phase_turns = ((child_value - 0.5) * 0.5 + 0.25 * cheb_points[:, None] - 0.5 * cheb_points[None, :]) * (box_ratio * (side_value - 0.5) * 0.5)
    radians = 2.0 * jnp.pi * phase_turns
    return weights * (jnp.cos(radians) + jnp.sin(radians))

def initial_coefficients(sample_block, labels, corner_x, corner_y):
    size_x, size_y, records = sample_block.shape
    flattened = sample_block.reshape(size_x * size_y, records)
    group_size = min(FB, max(1, 512 // (Q1 * Q2)))
    width_x = N // (2 * size_x)
    width_y = N // (2 * size_y)
    nodes_x = cheb_nodes(Q1)
    nodes_y = cheb_nodes(Q2)
    offset_x = jnp.arange(size_x, dtype=jnp.float32)
    offset_y = jnp.arange(size_y, dtype=jnp.float32)

    def one_group(labels_group):
        label_x = labels_group // FBY
        label_y = labels_group % FBY
        centre_x = label_x * width_x + width_x // 2
        centre_y = label_y * width_y + width_y // 2
        corner_turns = ((corner_x * centre_x + corner_y * centre_y) % N).astype(jnp.float32)
        points_x = centre_x.astype(jnp.float32)[:, None] + 0.5 * width_x * nodes_x[None, :]
        points_y = centre_y.astype(jnp.float32)[:, None] + 0.5 * width_y * nodes_y[None, :]
        phase_turns = (corner_turns[:, None, None, None, None] + points_x[:, :, None, None, None] * offset_x[None, None, None, :, None] + points_y[:, None, :, None, None] * offset_y[None, None, None, None, :]) / N
        radians = 2.0 * jnp.pi * phase_turns
        cas_table = (jnp.cos(radians) + jnp.sin(radians)).astype(jnp.bfloat16)
        cas_table = cas_table.reshape(labels_group.shape[0] * Q1 * Q2, size_x * size_y)
        return jnp.dot(cas_table, flattened, preferred_element_type=jnp.float32)
    blocks = lax.map(one_group, labels.reshape(FB // group_size, group_size))
    norm_scale = 1.0 / math.sqrt(size_x * size_y)
    return (blocks * norm_scale).reshape(FB, Q1, Q2, records)

def reference(samples, box_labels):
    devices_total = N_GX * N_GY

    def one_device(device):
        device_x = device // N_GY
        device_y = device % N_GY
        sample_block = lax.dynamic_slice(samples, (device_x * BX, device_y * BY, jnp.int32(0)), (BX, BY, V))
        return initial_coefficients(sample_block, box_labels, device_x * BX, device_y * BY)
    initial = lax.map(one_device, jnp.arange(devices_total, dtype=jnp.int32))
    initial = initial.reshape(N_GX, N_GY, FB, Q1, Q2, V)
    ratio_x = 2.0 * BX * (N // (2 * BX)) / N
    ratio_y = 2.0 * BY * (N // (2 * BY)) / N
    side_list = [g // (N_GX // 2) for g in range(N_GX)]
    own_x = jnp.stack([level_matrix(Q1, ratio_x, s, s) for s in side_list])
    cross_x = jnp.stack([level_matrix(Q1, ratio_x, 1 - s, s) for s in side_list])
    partner = jnp.roll(initial, N_GX // 2, axis=0)
    merged_x = jnp.einsum('gpq,gyaqjv->gyapjv', own_x, initial, precision=lax.Precision.HIGHEST) + jnp.einsum('gpq,gyaqjv->gyapjv', cross_x, partner, precision=lax.Precision.HIGHEST)
    side_list = [g // (N_GY // 2) for g in range(N_GY)]
    own_y = jnp.stack([level_matrix(Q2, ratio_y, s, s) for s in side_list])
    cross_y = jnp.stack([level_matrix(Q2, ratio_y, 1 - s, s) for s in side_list])
    partner = jnp.roll(merged_x, N_GY // 2, axis=1)
    merged_y = jnp.einsum('ypq,gyaiqv->gyaipv', own_y, merged_x, precision=lax.Precision.HIGHEST) + jnp.einsum('ypq,gyaiqv->gyaipv', cross_y, partner, precision=lax.Precision.HIGHEST)
    return merged_y.reshape(N_GX, N_GY, FB * Q1 * Q2, V)
```

```python
import functools
import math

import jax
import jax.numpy as jnp
import numpy as np
from jax import lax
from jax.experimental import pallas as pl
from jax.experimental.pallas import tpu as pltpu
from jax.sharding import PartitionSpec as P

N = 16384
FBY = 4
FB = 16
Q1 = 8
Q2 = 16
Q = Q1 * Q2
LANES = 256
GROUPS = (1, 2, 4, 5, 3, 1)
VMEM = 48 << 20


def cheb_nodes(points):
    return np.cos(np.pi * (2.0 * np.arange(points) + 1.0) / (2.0 * points))


def level_matrix(points, box_ratio, side, child):
    nodes = cheb_nodes(points)
    targets = child - 0.5 + 0.5 * nodes
    weights = np.ones((points, points))
    for m in range(points):
        for other in range(points):
            if other != m:
                weights[:, m] *= (targets - nodes[other]) / (nodes[m] - nodes[other])
    turns = ((child - 0.5) * 0.5 + 0.25 * nodes[:, None] - 0.5 * nodes[None, :]) * (box_ratio * (side - 0.5) * 0.5)
    radians = 2.0 * np.pi * turns
    return weights * (np.cos(radians) + np.sin(radians))


def level_tables(points, box_ratio, spread, scale):
    both = np.stack(
        [
            np.concatenate([spread(level_matrix(points, box_ratio, s, c)) for c in (s, 1 - s)], axis=0)
            for s in (0, 1)
        ]
    )
    both = (both * scale).astype(np.float32)
    high = both.astype(jnp.bfloat16)
    low = (both - high.astype(np.float32)).astype(jnp.bfloat16)
    return jnp.asarray(high), jnp.asarray(low)


def product(high, low, value):
    value_high = value.astype(jnp.bfloat16)
    value_low = (value - value_high.astype(jnp.float32)).astype(jnp.bfloat16)
    dot = functools.partial(jnp.dot, preferred_element_type=jnp.float32)
    return dot(high, value_high) + (dot(low, value_high) + dot(high, value_low))


def node_column(points):
    counter = lax.broadcasted_iota(jnp.int32, (points, 1), 0).astype(jnp.float32)
    return jnp.cos(jnp.pi * (2.0 * counter + 1.0) / (2.0 * points))


def first_kernel(first_slot, slots, size_x, size_y, labels, place, x_ref, high_ref, low_ref, out_ref, kept_ref, spread_ref, cos_ref, sin_ref, table_ref):
    width_x, width_y = N // (2 * size_x), N // (2 * size_y)
    samples_box = size_x * size_y

    @pl.when(pl.program_id(0) == 0)
    def _():
        owner = lax.broadcasted_iota(jnp.int32, (size_x, samples_box), 1) // size_y
        row = lax.broadcasted_iota(jnp.int32, (size_x, samples_box), 0)
        spread_ref[...] = (owner == row).astype(jnp.float32).astype(jnp.bfloat16)
        steps_x = lax.broadcasted_iota(jnp.int32, (Q1, size_x), 1).astype(jnp.float32)
        steps_y = (lax.broadcasted_iota(jnp.int32, (Q2, 2 * size_y), 1) % size_y).astype(jnp.float32)
        nodes_x, nodes_y = node_column(Q1), node_column(Q2)

        def build(slot, _):
            label = labels[first_slot + slot]
            centre_x = (label // FBY) * width_x + width_x // 2
            centre_y = (label % FBY) * width_y + width_y // 2
            corner = ((place[0] * centre_x + place[1] * centre_y) % N).astype(jnp.float32)
            points_x = centre_x.astype(jnp.float32) + 0.5 * width_x * nodes_x
            points_y = centre_y.astype(jnp.float32) + 0.5 * width_y * nodes_y
            angle_x = 2.0 * jnp.pi * ((corner + points_x * steps_x) / N)
            angle_y = 2.0 * jnp.pi * ((points_y * steps_y) / N)
            cos_y, sin_y = jnp.cos(angle_y), jnp.sin(angle_y)
            plus_y, minus_y = cos_y + sin_y, cos_y - sin_y
            parts = jnp.concatenate([jnp.cos(angle_x), jnp.sin(angle_x)], axis=0)
            parts_high = parts.astype(jnp.bfloat16).astype(jnp.float32)
            stacked = jnp.concatenate([parts_high, parts - parts_high], axis=0).astype(jnp.bfloat16)
            wide = jnp.dot(stacked, spread_ref[...], preferred_element_type=jnp.float32)
            cos_ref[...] = wide[:Q1] + wide[2 * Q1 : 3 * Q1]
            sin_ref[...] = wide[Q1 : 2 * Q1] + wide[3 * Q1 :]
            for at in range(0, samples_box, 2 * size_y):
                for i in range(Q1):
                    cos_x = cos_ref[i : i + 1, at : at + 2 * size_y]
                    sin_x = sin_ref[i : i + 1, at : at + 2 * size_y]
                    table_ref[slot, i * Q2 : (i + 1) * Q2, at : at + 2 * size_y] = (
                        cos_x * plus_y + sin_x * minus_y
                    ).astype(jnp.bfloat16)
            return 0

        lax.fori_loop(0, slots, build, 0)

    side = place[2]

    def apply(slot, _):
        initial = jnp.dot(table_ref[slot], x_ref[...].reshape(samples_box, LANES), preferred_element_type=jnp.float32)
        both = product(high_ref[side], low_ref[side], initial)
        kept_ref[slot] = both[:Q]
        out_ref[slot] = both[Q:]
        return 0

    lax.fori_loop(0, slots, apply, 0)


def first(labels, place, samples, tables, first_slot, slots, half):
    size_x, size_y, records = samples.shape
    samples_box = size_x * size_y
    blocks = records // 2 // LANES
    smem = pl.BlockSpec(memory_space=pltpu.SMEM)
    whole = pl.BlockSpec((2, 2 * Q, Q), lambda j: (0, 0, 0))
    made = pl.BlockSpec((slots, Q, LANES), lambda j: (0, 0, j))
    shape = jax.ShapeDtypeStruct((slots, Q, records // 2), jnp.float32)
    return pl.pallas_call(
        functools.partial(first_kernel, first_slot, slots, size_x, size_y),
        grid=(blocks,),
        in_specs=[smem, smem, pl.BlockSpec((size_x, size_y, LANES), lambda j: (0, 0, half * blocks + j)), whole, whole],
        out_specs=[made, made],
        out_shape=[shape, shape],
        scratch_shapes=[
            pltpu.VMEM((size_x, samples_box), jnp.bfloat16),
            pltpu.VMEM((Q1, samples_box), jnp.float32),
            pltpu.VMEM((Q1, samples_box), jnp.float32),
            pltpu.VMEM((slots, Q, samples_box), jnp.bfloat16),
        ],
        compiler_params=pltpu.CompilerParams(vmem_limit_bytes=VMEM),
        cost_estimate=pl.CostEstimate(
            flops=4 * slots * Q * samples_box * records // 2, bytes_accessed=8 << 20, transcendentals=0
        ),
    )(labels, place, samples, *tables)


def second_kernel(place, kept_ref, came_ref, high_ref, low_ref, out_ref, left_ref):
    side = place[2]
    both = product(high_ref[side], low_ref[side], kept_ref[0] + came_ref[0])
    left_ref[0] = both[:Q]
    out_ref[0] = both[Q:]


def second(place, kept, came, tables):
    slots, _, lanes = kept.shape
    block = pl.BlockSpec((1, Q, lanes), lambda a: (a, 0, 0))
    whole = pl.BlockSpec((2, 2 * Q, Q), lambda a: (0, 0, 0))
    shape = jax.ShapeDtypeStruct(kept.shape, jnp.float32)
    return pl.pallas_call(
        second_kernel,
        grid=(slots,),
        in_specs=[pl.BlockSpec(memory_space=pltpu.SMEM), block, block, whole, whole],
        out_specs=[block, block],
        out_shape=[shape, shape],
        compiler_params=pltpu.CompilerParams(vmem_limit_bytes=VMEM),
        cost_estimate=pl.CostEstimate(
            flops=12 * slots * Q * Q * lanes, bytes_accessed=16 * slots * Q * lanes, transcendentals=0
        ),
    )(place, kept, came, *tables)


def third_kernel(left_a, came_a, left_b, came_b, *rest):
    total_ref = rest[-1]
    lanes = left_a.shape[-1]
    total_ref[0, :, :lanes] = left_a[0] + came_a[0]
    total_ref[0, :, lanes:] = left_b[0] + came_b[0]


def third(total, first_slot, left_a, came_a, left_b, came_b):
    slots, _, lanes = left_a.shape
    block = pl.BlockSpec((1, Q, lanes), lambda a: (a, 0, 0))
    given = [] if total is None else [total]
    return pl.pallas_call(
        third_kernel,
        grid=(slots,),
        in_specs=[block] * 4 + [pl.BlockSpec(memory_space=pl.ANY)] * len(given),
        out_specs=pl.BlockSpec((1, Q, 2 * lanes), lambda a: (first_slot + a, 0, 0)),
        out_shape=jax.ShapeDtypeStruct((FB, Q, 2 * lanes), jnp.float32),
        input_output_aliases={4: 0} if given else {},
        compiler_params=pltpu.CompilerParams(vmem_limit_bytes=VMEM),
        cost_estimate=pl.CostEstimate(
            flops=2 * slots * Q * lanes, bytes_accessed=24 * slots * Q * lanes, transcendentals=0
        ),
    )(left_a, came_a, left_b, came_b, *given)


def swapped(x, axis):
    size = lax.axis_size(axis)
    return lax.ppermute(x, axis, [(i, (i + size // 2) % size) for i in range(size)])


def local(samples, box_labels):
    size_x, size_y, records = samples.shape
    device_x, device_y = lax.axis_index("gx"), lax.axis_index("gy")
    side_x = device_x // (lax.axis_size("gx") // 2)
    side_y = device_y // (lax.axis_size("gy") // 2)
    corner = (device_x * size_x, device_y * size_y)
    place_x = jnp.stack([*corner, side_x]).astype(jnp.int32)
    place_y = jnp.stack([*corner, side_y]).astype(jnp.int32)
    ratio_x = 2.0 * size_x * (N // (2 * size_x)) / N
    ratio_y = 2.0 * size_y * (N // (2 * size_y)) / N
    norm = 1.0 / math.sqrt(size_x * size_y)
    spread_x = lambda g: np.kron(g, np.eye(Q2))
    spread_y = lambda g: np.kron(np.eye(Q1), g)
    first_x = level_tables(Q1, ratio_x, spread_x, norm)
    first_y = level_tables(Q2, ratio_y, spread_y, norm)
    second_x = level_tables(Q1, ratio_x, spread_x, 1.0)
    second_y = level_tables(Q2, ratio_y, spread_y, 1.0)

    starts = [sum(GROUPS[:g]) for g in range(len(GROUPS))]
    ones = []
    for at, slots in zip(starts, GROUPS):
        out_a, kept_a = first(box_labels, place_x, samples, first_x, at, slots, 0)
        came_a = swapped(out_a, "gx")
        out_b, kept_b = first(box_labels, place_y, samples, first_y, at, slots, 1)
        came_b = swapped(out_b, "gy")
        ones.append((kept_a, came_a, kept_b, came_b))
    twos = []
    for kept_a, came_a, kept_b, came_b in ones:
        out_a, left_a = second(place_y, kept_a, came_a, second_y)
        came_a = swapped(out_a, "gy")
        out_b, left_b = second(place_x, kept_b, came_b, second_x)
        came_b = swapped(out_b, "gx")
        twos.append((left_a, came_a, left_b, came_b))
    total = None
    for at, two in zip(starts, twos):
        total = third(total, at, *two)
    return total.reshape(1, 1, FB * Q, records)


def solution(mesh):
    in_specs = (P("gx", "gy", None), P())
    out_specs = P("gx", "gy", None, None)
    return jax.shard_map(local, mesh=mesh, in_specs=in_specs, out_specs=out_specs, check_vma=False)
```

```python
import functools
import math

import jax
import jax.numpy as jnp
import numpy as np
from jax import lax
from jax.experimental import pallas as pl
from jax.experimental.pallas import tpu as pltpu
from jax.sharding import PartitionSpec as P

N = 16384
FBY = 4
FB = 16
Q1 = 8
Q2 = 16
Q = Q1 * Q2
LANES = 256
MESH = pl.DeviceIdType.MESH


def cheb_nodes(points):
    return np.cos(np.pi * (2.0 * np.arange(points) + 1.0) / (2.0 * points))


def level_matrix(points, box_ratio, side, child):
    nodes = cheb_nodes(points)
    targets = child - 0.5 + 0.5 * nodes
    weights = np.ones((points, points))
    for m in range(points):
        for other in range(points):
            if other != m:
                weights[:, m] *= (targets - nodes[other]) / (nodes[m] - nodes[other])
    turns = ((child - 0.5) * 0.5 + 0.25 * nodes[:, None] - 0.5 * nodes[None, :]) * (box_ratio * (side - 0.5) * 0.5)
    radians = 2.0 * np.pi * turns
    return weights * (np.cos(radians) + np.sin(radians))


def level_tables(points, box_ratio, spread):
    both = np.stack(
        [
            np.concatenate([spread(level_matrix(points, box_ratio, s, c)) for c in (s, 1 - s)], axis=0)
            for s in (0, 1)
        ]
    ).astype(np.float32)
    high = both.astype(jnp.bfloat16)
    low = (both - high.astype(np.float32)).astype(jnp.bfloat16)
    return np.stack([high, low], axis=1)


def product(tables, value):
    high, low = tables[0], tables[1]
    value_high = value.astype(jnp.bfloat16)
    value_low = (value - value_high.astype(jnp.float32)).astype(jnp.bfloat16)
    dot = functools.partial(jnp.dot, preferred_element_type=jnp.float32)
    return dot(high, value_high) + (dot(low, value_high) + dot(high, value_low))


def node_column(points):
    counter = lax.broadcasted_iota(jnp.int32, (points, 1), 0).astype(jnp.float32)
    return jnp.cos(jnp.pi * (2.0 * counter + 1.0) / (2.0 * points))


def kernel(
    labels, samples, level_consts, total,
    x_ref, levels, spread, wide, table, sent, came, last,
    x_sem, level_sem, send_sem, came_sem, resend_sem, last_sem,
):
    size_x, size_y, records = samples.shape
    samples_box = size_x * size_y
    width_x, width_y = N // (2 * size_x), N // (2 * size_y)
    norm = 1.0 / math.sqrt(samples_box)
    half = records // 2
    blocks = records // LANES
    count_x, count_y = lax.axis_size("gx"), lax.axis_size("gy")
    device_x, device_y = lax.axis_index("gx"), lax.axis_index("gy")
    partners = (
        (lax.rem(device_x + count_x // 2, count_x), device_y),
        (device_x, lax.rem(device_y + count_y // 2, count_y)),
    )
    sides = (device_x // (count_x // 2), device_y // (count_y // 2))

    barrier = pltpu.get_barrier_semaphore()
    for partner in partners:
        pl.semaphore_signal(barrier, inc=1, device_id=partner, device_id_type=MESH)

    def load_block(j):
        lanes = pl.ds(j * LANES, LANES)
        return pltpu.make_async_copy(samples.at[:, :, lanes], x_ref.at[:, :, lanes], x_sem.at[j])

    def load_level(axis):
        return pltpu.make_async_copy(level_consts.at[axis, sides[axis]], levels.at[axis], level_sem.at[axis])

    load_block(0).start()
    for axis in range(2):
        load_level(axis).start()
    for j in range(1, blocks):
        load_block(j).start()

    owner = lax.broadcasted_iota(jnp.int32, (size_x, samples_box), 1) // size_y
    row = lax.broadcasted_iota(jnp.int32, (size_x, samples_box), 0)
    spread[...] = (owner == row).astype(jnp.float32).astype(jnp.bfloat16)
    steps_x = lax.broadcasted_iota(jnp.int32, (Q1, size_x), 1).astype(jnp.float32)
    steps_y = (lax.broadcasted_iota(jnp.int32, (Q2, 2 * size_y), 1) % size_y).astype(jnp.float32)
    nodes_x, nodes_y = node_column(Q1), node_column(Q2)

    def build_table(slot):
        label = labels[slot]
        centre_x = (label // FBY) * width_x + width_x // 2
        centre_y = (label % FBY) * width_y + width_y // 2
        corner = ((device_x * size_x * centre_x + device_y * size_y * centre_y) % N).astype(jnp.float32)
        points_x = centre_x.astype(jnp.float32) + 0.5 * width_x * nodes_x
        points_y = centre_y.astype(jnp.float32) + 0.5 * width_y * nodes_y
        angle_x = 2.0 * jnp.pi * ((corner + points_x * steps_x) / N)
        angle_y = 2.0 * jnp.pi * ((points_y * steps_y) / N)
        cos_y, sin_y = jnp.cos(angle_y), jnp.sin(angle_y)
        plus_y, minus_y = cos_y + sin_y, cos_y - sin_y
        parts = jnp.concatenate([jnp.cos(angle_x), jnp.sin(angle_x)], axis=0)
        parts_high = parts.astype(jnp.bfloat16).astype(jnp.float32)
        stacked = jnp.concatenate([parts_high, parts - parts_high], axis=0).astype(jnp.bfloat16)
        expanded = jnp.dot(stacked, spread[...], preferred_element_type=jnp.float32)
        wide[...] = expanded[: 2 * Q1] + expanded[2 * Q1 :]
        pair = 2 * size_y
        run = 4 * pair

        def fill(step, _):
            for i in range(Q1):
                for at in range(0, run, pair):
                    lanes = pl.ds(pl.multiple_of(step * run, run) + at, pair)
                    cos_x, sin_x = wide[i : i + 1, lanes], wide[Q1 + i : Q1 + i + 1, lanes]
                    table[i * Q2 : (i + 1) * Q2, lanes] = (cos_x * plus_y + sin_x * minus_y).astype(jnp.bfloat16)
            return 0

        lax.fori_loop(0, samples_box // run, fill, 0)

    def send(axis, slot):
        return pltpu.make_async_remote_copy(
            src_ref=sent.at[axis, slot], dst_ref=came.at[axis, slot],
            send_sem=send_sem.at[axis, slot], recv_sem=came_sem.at[axis, slot],
            device_id=partners[axis], device_id_type=MESH,
        )

    def resend(axis, slot):
        return pltpu.make_async_remote_copy(
            src_ref=came.at[axis, slot], dst_ref=last.at[axis, slot],
            send_sem=resend_sem.at[axis, slot], recv_sem=last_sem.at[axis, slot],
            device_id=partners[1 - axis], device_id_type=MESH,
        )

    def first(slot, _):
        build_table(slot)
        for j in range(blocks):
            axis = j // (blocks // 2)

            @pl.when(slot == 0)
            def _(j=j, axis=axis):
                load_block(j).wait()
                if j % (blocks // 2) == 0:
                    load_level(axis).wait()

            lanes = slice(j * LANES, (j + 1) * LANES)
            within = slice(j * LANES - axis * half, (j + 1) * LANES - axis * half)
            block = x_ref[:, :, lanes].reshape(samples_box, LANES)
            initial = norm * jnp.dot(table[...], block, preferred_element_type=jnp.float32)
            both = product(levels.at[axis], initial)
            total[slot, :, lanes] = both[:Q]
            sent[axis, slot, :, within] = both[Q:]
            if j % (blocks // 2) == blocks // 2 - 1:
                if axis == 0:

                    @pl.when(slot == 0)
                    def _():
                        pl.semaphore_wait(barrier, 2)

                send(axis, slot).start()
        return 0

    lax.fori_loop(0, FB, first, 0)

    def second(slot, _):
        for axis in range(2):
            lanes = slice(axis * half, (axis + 1) * half)
            send(axis, slot).wait_recv()
            both = product(levels.at[1 - axis], total[slot, :, lanes] + came[axis, slot])
            total[slot, :, lanes] = both[:Q]
            came[axis, slot] = both[Q:]
            resend(axis, slot).start()
        return 0

    lax.fori_loop(0, FB, second, 0)

    def third(slot, _):
        for axis in range(2):
            lanes = slice(axis * half, (axis + 1) * half)
            send(axis, slot).wait_send()
            resend(axis, slot).wait()
            total[slot, :, lanes] += last[axis, slot]
        return 0

    lax.fori_loop(0, FB, third, 0)


def local(samples, box_labels):
    size_x, size_y, records = samples.shape
    ratio_x = 2.0 * size_x * (N // (2 * size_x)) / N
    ratio_y = 2.0 * size_y * (N // (2 * size_y)) / N
    consts = np.stack(
        [
            level_tables(Q1, ratio_x, lambda g: np.kron(g, np.eye(Q2))),
            level_tables(Q2, ratio_y, lambda g: np.kron(np.eye(Q1), g)),
        ]
    )
    half = records // 2
    held = pltpu.VMEM((2, FB, Q, half), jnp.float32)
    sems = pltpu.SemaphoreType.DMA((2, FB))
    total = pl.pallas_call(
        kernel,
        in_specs=[
            pl.BlockSpec(memory_space=pltpu.SMEM),
            pl.BlockSpec(memory_space=pl.ANY),
            pl.BlockSpec(memory_space=pl.ANY),
        ],
        out_specs=pl.BlockSpec(memory_space=pltpu.VMEM),
        out_shape=pltpu.VMEM((FB, Q, records), jnp.float32),
        scratch_shapes=[
            pltpu.VMEM(samples.shape, jnp.bfloat16),
            pltpu.VMEM((2, 2, 2 * Q, Q), jnp.bfloat16),
            pltpu.VMEM((size_x, size_x * size_y), jnp.bfloat16),
            pltpu.VMEM((2 * Q1, size_x * size_y), jnp.float32),
            pltpu.VMEM((Q, size_x * size_y), jnp.bfloat16),
            held, held, held,
            pltpu.SemaphoreType.DMA((records // LANES,)),
            pltpu.SemaphoreType.DMA((2,)),
            sems, sems, sems, sems,
        ],
        compiler_params=pltpu.CompilerParams(collective_id=0, has_side_effects=True, vmem_limit_bytes=46 << 20),
    )(box_labels, samples, jnp.asarray(consts))
    return total.reshape(1, 1, FB * Q, records)


def solution(mesh):
    in_specs = (P("gx", "gy", None), P())
    out_specs = P("gx", "gy", None, None)
    return jax.shard_map(local, mesh=mesh, in_specs=in_specs, out_specs=out_specs, check_vma=False)
```

```python
import functools
import math

import jax
import jax.numpy as jnp
import numpy as np
from jax import lax
from jax.experimental import pallas as pl
from jax.experimental.pallas import tpu as pltpu
from jax.sharding import PartitionSpec as P

N = 16384
FBY = 4
FB = 16
Q1 = 8
Q2 = 16
Q = Q1 * Q2
LANES = 512
FINE = 256
MESH = pl.DeviceIdType.MESH
SENDS = ((1, 1), (2, 1), (3, 1), (4, 1), (5, 1), (6, 1), (7, 1), (8, 1), (9, 1), (10, 1), (11, 1), (12, 1), (13, 1), (14, 1), (15, 1))
RESENDS = ((0, 1), (1, 1), (2, 1), (3, 1), (4, 1), (5, 1), (6, 1), (7, 1), (8, 1), (9, 1), (10, 1), (11, 1), (12, 1), (13, 1), (14, 1), (15, 1))
FLIGHT = 16


def cheb_nodes(points):
    return np.cos(np.pi * (2.0 * np.arange(points) + 1.0) / (2.0 * points))


def level_matrix(points, box_ratio, side, child):
    nodes = cheb_nodes(points)
    targets = child - 0.5 + 0.5 * nodes
    weights = np.ones((points, points))
    for m in range(points):
        for other in range(points):
            if other != m:
                weights[:, m] *= (targets - nodes[other]) / (nodes[m] - nodes[other])
    turns = ((child - 0.5) * 0.5 + 0.25 * nodes[:, None] - 0.5 * nodes[None, :]) * (box_ratio * (side - 0.5) * 0.5)
    radians = 2.0 * np.pi * turns
    return weights * (np.cos(radians) + np.sin(radians))


def level_tables(points, box_ratio, spread):
    both = np.stack(
        [
            np.concatenate([spread(level_matrix(points, box_ratio, s, c)) for c in (s, 1 - s)], axis=0)
            for s in (0, 1)
        ]
    ).astype(np.float32)
    high = both.astype(jnp.bfloat16)
    low = (both - high.astype(np.float32)).astype(jnp.bfloat16)
    return np.stack([high, low], axis=1)


def product(tables, value):
    high, low = tables[0], tables[1]
    value_high = value.astype(jnp.bfloat16)
    value_low = (value - value_high.astype(jnp.float32)).astype(jnp.bfloat16)
    dot = functools.partial(jnp.dot, preferred_element_type=jnp.float32)
    return dot(high, value_high) + (dot(low, value_high) + dot(high, value_low))


def kernel(
    labels_in, samples, level_consts, total,
    labels, x_ref, levels, spread, wide, narrow, table, sent, came, last,
    label_sem, x_sem, level_sem, send_sem, came_sem, resend_sem, last_sem,
):
    size_x, size_y, records = samples.shape
    samples_box = size_x * size_y
    width_x, width_y = N // (2 * size_x), N // (2 * size_y)
    norm = 1.0 / math.sqrt(samples_box)
    half = records // 2
    blocks, fine = records // LANES, records // FINE
    count_x, count_y = lax.axis_size("gx"), lax.axis_size("gy")
    device_x, device_y = lax.axis_index("gx"), lax.axis_index("gy")
    partners = (
        (lax.rem(device_x + count_x // 2, count_x), device_y),
        (device_x, lax.rem(device_y + count_y // 2, count_y)),
    )
    sides = (device_x // (count_x // 2), device_y // (count_y // 2))
    order = [axis * (fine // 2) + k for k in range(fine // 2) for axis in (1, 0)]

    barrier = pltpu.get_barrier_semaphore()
    for partner in partners:
        pl.semaphore_signal(barrier, inc=1, device_id=partner, device_id_type=MESH)

    def load_block(j):
        lanes = pl.ds(j * FINE, FINE)
        return pltpu.make_async_copy(samples.at[:, :, lanes], x_ref.at[:, :, lanes], x_sem.at[j])

    def load_level(axis):
        return pltpu.make_async_copy(level_consts.at[axis, sides[axis]], levels.at[axis], level_sem.at[axis])

    load_labels = pltpu.make_async_copy(labels_in, labels, label_sem)
    load_labels.start()
    load_block(order[0]).start()
    for axis in range(2):
        load_level(axis).start()
    for j in order[1:]:
        load_block(j).start()

    boxes_x = FB // FBY
    column = lax.broadcasted_iota(jnp.int32, (size_x, samples_box), 1)
    first_column = size_y * lax.broadcasted_iota(jnp.int32, (size_x, samples_box), 0)
    inside = (column >= first_column) & (column < first_column + size_y)
    spread[...] = jnp.where(inside, 1.0, 0.0).astype(jnp.bfloat16)
    row = lax.broadcasted_iota(jnp.int32, (boxes_x * Q1, 1), 0)
    centre = (row // Q1) * width_x + width_x // 2
    node = jnp.cos(jnp.pi * (2.0 * (row % Q1).astype(jnp.float32) + 1.0) / (2.0 * Q1))
    corner = ((device_x * size_x * centre) % N).astype(jnp.float32)
    step = lax.broadcasted_iota(jnp.int32, (boxes_x * Q1, size_x), 1).astype(jnp.float32)
    angle = 2.0 * jnp.pi * ((corner + (centre.astype(jnp.float32) + 0.5 * width_x * node) * step) / N)
    parts = jnp.concatenate([jnp.cos(angle), jnp.sin(angle)], axis=0)
    parts_high = parts.astype(jnp.bfloat16).astype(jnp.float32)
    for k, part in enumerate((parts_high, parts - parts_high)):
        repeated = jnp.dot(part.astype(jnp.bfloat16), spread[...], preferred_element_type=jnp.float32)
        repeated = repeated.reshape(2, boxes_x, Q1, samples_box)
        if k == 0:
            wide[...] = repeated
        else:
            wide[...] += repeated

    row = lax.broadcasted_iota(jnp.int32, (FBY * Q2, 1), 0)
    centre = (row // Q2) * width_y + width_y // 2
    node = jnp.cos(jnp.pi * (2.0 * (row % Q2).astype(jnp.float32) + 1.0) / (2.0 * Q2))
    corner = ((device_y * size_y * centre) % N).astype(jnp.float32)
    step = (lax.broadcasted_iota(jnp.int32, (FBY * Q2, 2 * size_y), 1) % size_y).astype(jnp.float32)
    angle = 2.0 * jnp.pi * ((corner + (centre.astype(jnp.float32) + 0.5 * width_y * node) * step) / N)
    narrow[0] = (jnp.cos(angle) + jnp.sin(angle)).reshape(FBY, Q2, 2 * size_y)
    narrow[1] = (jnp.cos(angle) - jnp.sin(angle)).reshape(FBY, Q2, 2 * size_y)
    load_labels.wait()

    def build_table(slot):
        label_x, label_y = labels[slot] // FBY, labels[slot] % FBY
        plus_y, minus_y = narrow[0, label_y], narrow[1, label_y]
        pair = 2 * size_y
        run = 4 * pair

        def fill(k, _):
            for i in range(Q1):
                for at in range(0, run, pair):
                    lanes = pl.ds(pl.multiple_of(k * run, run) + at, pair)
                    cos_x, sin_x = wide[0, label_x, i : i + 1, lanes], wide[1, label_x, i : i + 1, lanes]
                    table[i * Q2 : (i + 1) * Q2, lanes] = (cos_x * plus_y + sin_x * minus_y).astype(jnp.bfloat16)
            return 0

        lax.fori_loop(0, samples_box // run, fill, 0)

    whole = [(start, slots, 0, half) for start, slots in SENDS]
    pieces = [(0, 1, at, FINE) for at in range(0, half, FINE)]
    sends = pieces + whole
    resends = [(start, slots, 0, half) for start, slots in RESENDS]

    def view(ref, axis, message):
        start, slots, at, width = message
        return ref.at[axis, pl.ds(start, slots), :, pl.ds(at, width)]

    def send(axis, k):
        return pltpu.make_async_remote_copy(
            src_ref=view(sent, axis, sends[k]), dst_ref=view(came, axis, sends[k]),
            send_sem=send_sem.at[axis, k], recv_sem=came_sem.at[axis, k],
            device_id=partners[axis], device_id_type=MESH,
        )

    def resend(axis, k):
        return pltpu.make_async_remote_copy(
            src_ref=view(came, axis, resends[k]), dst_ref=view(last, axis, resends[k]),
            send_sem=resend_sem.at[axis, k], recv_sem=last_sem.at[axis, k],
            device_id=partners[1 - axis], device_id_type=MESH,
        )

    def at_end(messages, slot, act, skip=0):
        for k, (start, slots, _, _) in enumerate(messages):
            if k >= skip:
                pl.when(slot == start + slots - 1)(functools.partial(act, k))

    def at_start(messages, slot, act):
        for k, (start, _, _, _) in enumerate(messages):
            pl.when(slot == start)(functools.partial(act, k))

    def start_send(axis, k):
        if k >= FLIGHT:
            send(axis, k - FLIGHT).wait_send()
        send(axis, k).start()

    def start_resend(axis, k):
        if k >= FLIGHT:
            resend(axis, k - FLIGHT).wait_send()
        else:
            send(1 - axis, len(sends) + k - FLIGHT).wait_send()
        resend(axis, k).start()

    def first_level(axis, slot, at, width):
        lanes = slice(axis * half + at, axis * half + at + width)
        block = x_ref[:, :, lanes].reshape(samples_box, width)
        initial = norm * jnp.dot(table[...], block, preferred_element_type=jnp.float32)
        both = product(levels.at[axis], initial)
        total[slot, :, lanes] = both[:Q]
        sent[axis, slot, :, at : at + width] = both[Q:]

    build_table(0)
    for at, j in enumerate(order):
        axis, k = j // (fine // 2), j % (fine // 2)
        load_block(j).wait()
        if at < 2:
            load_level(axis).wait()
        first_level(axis, 0, k * FINE, FINE)
        if at == 0:
            pl.semaphore_wait(barrier, 2)
        start_send(axis, k)

    def first(slot, _):
        build_table(slot)
        for axis in (1, 0):
            for at in range(0, half, LANES):
                first_level(axis, slot, at, LANES)
            at_end(sends, slot, functools.partial(start_send, axis), len(pieces))
        return 0

    lax.fori_loop(1, FB, first, 0)

    def second(slot, _):
        for axis in (1, 0):
            lanes = slice(axis * half, (axis + 1) * half)
            at_start(sends, slot, lambda k, axis=axis: send(axis, k).wait_recv())
            both = product(levels.at[1 - axis], total[slot, :, lanes] + came[axis, slot])
            total[slot, :, lanes] = both[:Q]
            came[axis, slot] = both[Q:]
            at_end(resends, slot, functools.partial(start_resend, axis))
        return 0

    lax.fori_loop(0, FB, second, 0)

    def third(slot, _):
        for axis in (1, 0):
            lanes = slice(axis * half, (axis + 1) * half)
            at_start(resends, slot, lambda k, axis=axis: resend(axis, k).wait_recv())
            total[slot, :, lanes] += last[axis, slot]
        return 0

    lax.fori_loop(0, FB, third, 0)
    for axis in (1, 0):
        for k in range(len(resends) - FLIGHT, len(resends)):
            resend(axis, k).wait_send()


def local(samples, box_labels):
    size_x, size_y, records = samples.shape
    ratio_x = 2.0 * size_x * (N // (2 * size_x)) / N
    ratio_y = 2.0 * size_y * (N // (2 * size_y)) / N
    consts = np.stack(
        [
            level_tables(Q1, ratio_x, lambda g: np.kron(g, np.eye(Q2))),
            level_tables(Q2, ratio_y, lambda g: np.kron(np.eye(Q1), g)),
        ]
    )
    half = records // 2
    held = pltpu.VMEM((2, FB, Q, half), jnp.float32)
    sems = pltpu.SemaphoreType.DMA((2, FB + half // FINE))
    total = pl.pallas_call(
        kernel,
        in_specs=[
            pl.BlockSpec(memory_space=pl.ANY),
            pl.BlockSpec(memory_space=pl.ANY),
            pl.BlockSpec(memory_space=pl.ANY),
        ],
        out_specs=pl.BlockSpec(memory_space=pltpu.VMEM),
        out_shape=pltpu.VMEM((FB, Q, records), jnp.float32),
        scratch_shapes=[
            pltpu.SMEM(box_labels.shape, jnp.int32),
            pltpu.VMEM(samples.shape, jnp.bfloat16),
            pltpu.VMEM((2, 2, 2 * Q, Q), jnp.bfloat16),
            pltpu.VMEM((size_x, size_x * size_y), jnp.bfloat16),
            pltpu.VMEM((2, FB // FBY, Q1, size_x * size_y), jnp.float32),
            pltpu.VMEM((2, FBY, Q2, 2 * size_y), jnp.float32),
            pltpu.VMEM((Q, size_x * size_y), jnp.bfloat16),
            held, held, held,
            pltpu.SemaphoreType.DMA,
            pltpu.SemaphoreType.DMA((records // FINE,)),
            pltpu.SemaphoreType.DMA((2,)),
            sems, sems, sems, sems,
        ],
        compiler_params=pltpu.CompilerParams(collective_id=0, has_side_effects=True, vmem_limit_bytes=46 << 20),
    )(box_labels, samples, jnp.asarray(consts))
    return total.reshape(1, 1, FB * Q, records)


def solution(mesh):
    in_specs = (P("gx", "gy", None), P())
    out_specs = P("gx", "gy", None, None)
    return jax.shard_map(local, mesh=mesh, in_specs=in_specs, out_specs=out_specs, check_vma=False)
```

```python
import functools
import math

import jax
import jax.numpy as jnp
import numpy as np
from jax import lax
from jax.experimental import pallas as pl
from jax.experimental.pallas import tpu as pltpu
from jax.sharding import PartitionSpec as P

N = 16384
FBY = 4
FB = 16
Q1 = 8
Q2 = 16
Q = Q1 * Q2
LANES = 512
FINE = 256
MESH = pl.DeviceIdType.MESH
SENDS = ((1, 1), (2, 1), (3, 1), (4, 2), (6, 2), (8, 4), (12, 4))
RESENDS = ((0, 2), (2, 2), (4, 4), (8, 4), (12, 2), (14, 1), (15, 1))


def cheb_nodes(points):
    return np.cos(np.pi * (2.0 * np.arange(points) + 1.0) / (2.0 * points))


def level_matrix(points, box_ratio, side, child):
    nodes = cheb_nodes(points)
    targets = child - 0.5 + 0.5 * nodes
    weights = np.ones((points, points))
    for m in range(points):
        for other in range(points):
            if other != m:
                weights[:, m] *= (targets - nodes[other]) / (nodes[m] - nodes[other])
    turns = ((child - 0.5) * 0.5 + 0.25 * nodes[:, None] - 0.5 * nodes[None, :]) * (box_ratio * (side - 0.5) * 0.5)
    radians = 2.0 * np.pi * turns
    return weights * (np.cos(radians) + np.sin(radians))


def level_tables(points, box_ratio, spread):
    both = np.stack(
        [
            np.concatenate([spread(level_matrix(points, box_ratio, s, c)) for c in (s, 1 - s)], axis=0)
            for s in (0, 1)
        ]
    ).astype(np.float32)
    high = both.astype(jnp.bfloat16)
    low = (both - high.astype(np.float32)).astype(jnp.bfloat16)
    return np.stack([high, low], axis=1)


def product(tables, value):
    high, low = tables[0], tables[1]
    value_high = value.astype(jnp.bfloat16)
    value_low = (value - value_high.astype(jnp.float32)).astype(jnp.bfloat16)
    dot = functools.partial(jnp.dot, preferred_element_type=jnp.float32)
    return dot(high, value_high) + (dot(low, value_high) + dot(high, value_low))


def kernel(
    labels_in, samples, level_consts, total,
    labels, x_ref, levels, spread, wide, narrow, table, sent, came, last,
    label_sem, x_sem, level_sem, send_sem, came_sem, resend_sem, last_sem,
):
    size_x, size_y, records = samples.shape
    samples_box = size_x * size_y
    width_x, width_y = N // (2 * size_x), N // (2 * size_y)
    norm = 1.0 / math.sqrt(samples_box)
    half = records // 2
    blocks, fine = records // LANES, records // FINE
    count_x, count_y = lax.axis_size("gx"), lax.axis_size("gy")
    device_x, device_y = lax.axis_index("gx"), lax.axis_index("gy")
    partners = (
        (lax.rem(device_x + count_x // 2, count_x), device_y),
        (device_x, lax.rem(device_y + count_y // 2, count_y)),
    )
    sides = (device_x // (count_x // 2), device_y // (count_y // 2))
    order = [axis * (fine // 2) + k for k in range(fine // 2) for axis in (1, 0)]

    barrier = pltpu.get_barrier_semaphore()
    for partner in partners:
        pl.semaphore_signal(barrier, inc=1, device_id=partner, device_id_type=MESH)

    def load_block(j):
        lanes = pl.ds(j * FINE, FINE)
        return pltpu.make_async_copy(samples.at[:, :, lanes], x_ref.at[:, :, lanes], x_sem.at[j])

    def load_level(axis):
        return pltpu.make_async_copy(level_consts.at[axis, sides[axis]], levels.at[axis], level_sem)

    load_labels = pltpu.make_async_copy(labels_in, labels, label_sem)
    load_labels.start()
    load_block(order[0]).start()
    for axis in range(2):
        load_level(axis).start()
    for j in order[1:]:
        load_block(j).start()

    boxes_x = FB // FBY
    column = lax.broadcasted_iota(jnp.int32, (size_x, samples_box), 1)
    first_column = size_y * lax.broadcasted_iota(jnp.int32, (size_x, samples_box), 0)
    inside = (column >= first_column) & (column < first_column + size_y)
    spread[...] = jnp.where(inside, 1.0, 0.0).astype(jnp.bfloat16)
    row = lax.broadcasted_iota(jnp.int32, (boxes_x * Q1, 1), 0)
    centre = (row // Q1) * width_x + width_x // 2
    node = jnp.cos(jnp.pi * (2.0 * (row % Q1).astype(jnp.float32) + 1.0) / (2.0 * Q1))
    corner = ((device_x * size_x * centre) % N).astype(jnp.float32)
    step = lax.broadcasted_iota(jnp.int32, (boxes_x * Q1, size_x), 1).astype(jnp.float32)
    angle = 2.0 * jnp.pi * ((corner + (centre.astype(jnp.float32) + 0.5 * width_x * node) * step) / N)
    parts = jnp.concatenate([jnp.cos(angle), jnp.sin(angle)], axis=0)
    parts_high = parts.astype(jnp.bfloat16).astype(jnp.float32)
    for k, part in enumerate((parts_high, parts - parts_high)):
        repeated = jnp.dot(part.astype(jnp.bfloat16), spread[...], preferred_element_type=jnp.float32)
        repeated = repeated.reshape(2, boxes_x, Q1, samples_box)
        if k == 0:
            wide[...] = repeated
        else:
            wide[...] += repeated

    row = lax.broadcasted_iota(jnp.int32, (FBY * Q2, 1), 0)
    centre = (row // Q2) * width_y + width_y // 2
    node = jnp.cos(jnp.pi * (2.0 * (row % Q2).astype(jnp.float32) + 1.0) / (2.0 * Q2))
    corner = ((device_y * size_y * centre) % N).astype(jnp.float32)
    step = (lax.broadcasted_iota(jnp.int32, (FBY * Q2, 2 * size_y), 1) % size_y).astype(jnp.float32)
    angle = 2.0 * jnp.pi * ((corner + (centre.astype(jnp.float32) + 0.5 * width_y * node) * step) / N)
    narrow[0] = (jnp.cos(angle) + jnp.sin(angle)).reshape(FBY, Q2, 2 * size_y)
    narrow[1] = (jnp.cos(angle) - jnp.sin(angle)).reshape(FBY, Q2, 2 * size_y)
    load_labels.wait()

    def build_table(slot):
        label_x, label_y = labels[slot] // FBY, labels[slot] % FBY
        plus_y, minus_y = narrow[0, label_y], narrow[1, label_y]
        pair = 2 * size_y
        run = 4 * pair

        def fill(k, _):
            for i in range(Q1):
                for at in range(0, run, pair):
                    lanes = pl.ds(pl.multiple_of(k * run, run) + at, pair)
                    cos_x, sin_x = wide[0, label_x, i : i + 1, lanes], wide[1, label_x, i : i + 1, lanes]
                    table[i * Q2 : (i + 1) * Q2, lanes] = (cos_x * plus_y + sin_x * minus_y).astype(jnp.bfloat16)
            return 0

        lax.fori_loop(0, samples_box // run, fill, 0)

    whole = [(start, slots, 0, half) for start, slots in SENDS]
    pieces = [(0, 1, at, FINE) for at in range(0, half, FINE)]
    sends = pieces + whole
    resends = [(start, slots, 0, half) for start, slots in RESENDS]

    def view(ref, axis, message):
        start, slots, at, width = message
        return ref.at[axis, pl.ds(start, slots), :, pl.ds(at, width)]

    def send(axis, k):
        return pltpu.make_async_remote_copy(
            src_ref=view(sent, axis, sends[k]), dst_ref=view(came, axis, sends[k]),
            send_sem=send_sem.at[axis], recv_sem=came_sem.at[axis, k],
            device_id=partners[axis], device_id_type=MESH,
        )

    def resend(axis, k):
        return pltpu.make_async_remote_copy(
            src_ref=view(came, axis, resends[k]), dst_ref=view(last, axis, resends[k]),
            send_sem=resend_sem.at[axis], recv_sem=last_sem.at[axis, k],
            device_id=partners[1 - axis], device_id_type=MESH,
        )

    def at_end(messages, slot, act, skip=0):
        for k, (start, slots, _, _) in enumerate(messages):
            if k >= skip:
                pl.when(slot == start + slots - 1)(functools.partial(act, k))

    def at_start(messages, slot, act):
        for k, (start, _, _, _) in enumerate(messages):
            pl.when(slot == start)(functools.partial(act, k))

    def first_level(axis, slot, at, width):
        lanes = slice(axis * half + at, axis * half + at + width)
        block = x_ref[:, :, lanes].reshape(samples_box, width)
        initial = norm * jnp.dot(table[...], block, preferred_element_type=jnp.float32)
        both = product(levels.at[axis], initial)
        total[slot, :, lanes] = both[:Q]
        sent[axis, slot, :, at : at + width] = both[Q:]

    build_table(0)
    for at, j in enumerate(order):
        axis, k = j // (fine // 2), j % (fine // 2)
        load_block(j).wait()
        if at == 0:
            pltpu.make_async_copy(level_consts.at[:, 0], levels, level_sem).wait()
        first_level(axis, 0, k * FINE, FINE)
        if at == 0:
            pl.semaphore_wait(barrier, 2)
        send(axis, k).start()

    def first(slot, _):
        build_table(slot)
        for axis in (1, 0):
            for at in range(0, half, LANES):
                first_level(axis, slot, at, LANES)
            at_end(sends, slot, lambda k, axis=axis: send(axis, k).start(), len(pieces))
        return 0

    lax.fori_loop(1, FB, first, 0)

    def second(slot, _):
        for axis in (1, 0):
            lanes = slice(axis * half, (axis + 1) * half)
            at_start(sends, slot, lambda k, axis=axis: send(axis, k).wait_recv())
            both = product(levels.at[1 - axis], total[slot, :, lanes] + came[axis, slot])
            total[slot, :, lanes] = both[:Q]
            came[axis, slot] = both[Q:]
            at_end(resends, slot, lambda k, axis=axis: resend(axis, k).start())
        return 0

    lax.fori_loop(0, FB, second, 0)

    def third(slot, _):
        for axis in (1, 0):
            lanes = slice(axis * half, (axis + 1) * half)
            at_start(resends, slot, lambda k, axis=axis: resend(axis, k).wait_recv())
            total[slot, :, lanes] += last[axis, slot]
        return 0

    lax.fori_loop(0, FB, third, 0)
    for axis in range(2):
        for source, target, out_sem, in_sem in ((sent, came, send_sem, came_sem), (came, last, resend_sem, last_sem)):
            pltpu.make_async_remote_copy(
                src_ref=source.at[axis], dst_ref=target.at[axis],
                send_sem=out_sem.at[axis], recv_sem=in_sem.at[axis, 0],
                device_id=partners[axis], device_id_type=MESH,
            ).wait_send()


def local(samples, box_labels):
    size_x, size_y, records = samples.shape
    ratio_x = 2.0 * size_x * (N // (2 * size_x)) / N
    ratio_y = 2.0 * size_y * (N // (2 * size_y)) / N
    consts = np.stack(
        [
            level_tables(Q1, ratio_x, lambda g: np.kron(g, np.eye(Q2))),
            level_tables(Q2, ratio_y, lambda g: np.kron(np.eye(Q1), g)),
        ]
    )
    half = records // 2
    held = pltpu.VMEM((2, FB, Q, half), jnp.float32)
    pair = pltpu.SemaphoreType.DMA((2,))
    total = pl.pallas_call(
        kernel,
        in_specs=[
            pl.BlockSpec(memory_space=pl.ANY),
            pl.BlockSpec(memory_space=pl.ANY),
            pl.BlockSpec(memory_space=pl.ANY),
        ],
        out_specs=pl.BlockSpec(memory_space=pltpu.VMEM),
        out_shape=pltpu.VMEM((FB, Q, records), jnp.float32),
        scratch_shapes=[
            pltpu.SMEM(box_labels.shape, jnp.int32),
            pltpu.VMEM(samples.shape, jnp.bfloat16),
            pltpu.VMEM((2, 2, 2 * Q, Q), jnp.bfloat16),
            pltpu.VMEM((size_x, size_x * size_y), jnp.bfloat16),
            pltpu.VMEM((2, FB // FBY, Q1, size_x * size_y), jnp.float32),
            pltpu.VMEM((2, FBY, Q2, 2 * size_y), jnp.float32),
            pltpu.VMEM((Q, size_x * size_y), jnp.bfloat16),
            held, held, held,
            pltpu.SemaphoreType.DMA,
            pltpu.SemaphoreType.DMA((records // FINE,)),
            pltpu.SemaphoreType.DMA,
            pair, pltpu.SemaphoreType.DMA((2, half // FINE + len(SENDS))),
            pair, pltpu.SemaphoreType.DMA((2, len(RESENDS))),
        ],
        compiler_params=pltpu.CompilerParams(collective_id=0, has_side_effects=True, vmem_limit_bytes=46 << 20),
    )(box_labels, samples, jnp.asarray(consts))
    return total.reshape(1, 1, FB * Q, records)


def solution(mesh):
    in_specs = (P("gx", "gy", None), P())
    out_specs = P("gx", "gy", None, None)
    return jax.shard_map(local, mesh=mesh, in_specs=in_specs, out_specs=out_specs, check_vma=False)
```

```python
import functools
import math

import jax
import jax.numpy as jnp
import numpy as np
from jax import lax
from jax.experimental import pallas as pl
from jax.experimental.pallas import tpu as pltpu
from jax.sharding import PartitionSpec as P

N = 16384
FBY = 4
FB = 16
Q1 = 8
Q2 = 16
Q = Q1 * Q2
LANES = 512
PIECES = (256, 256)
MESH = pl.DeviceIdType.MESH
SENDS = ((1, 1), (2, 2), (4, 4), (8, 8))
RESENDS = ((0, 4), (4, 8), (12, 3), (15, 1))


def cheb_nodes(points):
    return np.cos(np.pi * (2.0 * np.arange(points) + 1.0) / (2.0 * points))


def level_matrix(points, box_ratio, side, child):
    nodes = cheb_nodes(points)
    targets = child - 0.5 + 0.5 * nodes
    weights = np.ones((points, points))
    for m in range(points):
        for other in range(points):
            if other != m:
                weights[:, m] *= (targets - nodes[other]) / (nodes[m] - nodes[other])
    turns = ((child - 0.5) * 0.5 + 0.25 * nodes[:, None] - 0.5 * nodes[None, :]) * (box_ratio * (side - 0.5) * 0.5)
    radians = 2.0 * np.pi * turns
    return weights * (np.cos(radians) + np.sin(radians))


def level_tables(points, box_ratio, spread):
    both = np.stack(
        [
            np.concatenate([spread(level_matrix(points, box_ratio, s, c)) for c in (s, 1 - s)], axis=0)
            for s in (0, 1)
        ]
    ).astype(np.float32)
    high = both.astype(jnp.bfloat16)
    low = (both - high.astype(np.float32)).astype(jnp.bfloat16)
    return np.stack([high, low], axis=1)


def product(tables, value):
    high, low = tables[0], tables[1]
    value_high = value.astype(jnp.bfloat16)
    value_low = (value - value_high.astype(jnp.float32)).astype(jnp.bfloat16)
    dot = functools.partial(jnp.dot, preferred_element_type=jnp.float32)
    return dot(high, value_high) + (dot(low, value_high) + dot(high, value_low))


def kernel(
    labels_in, samples, level_consts, total,
    labels, x_ref, levels, spread, wide, narrow, table, sent, came, last,
    label_sem, x_sem, level_sem, send_sem, came_sem, resend_sem, last_sem,
):
    size_x, size_y, records = samples.shape
    samples_box = size_x * size_y
    width_x, width_y = N // (2 * size_x), N // (2 * size_y)
    norm = 1.0 / math.sqrt(samples_box)
    half = records // 2
    count_x, count_y = lax.axis_size("gx"), lax.axis_size("gy")
    device_x, device_y = lax.axis_index("gx"), lax.axis_index("gy")
    partners = (
        (lax.rem(device_x + count_x // 2, count_x), device_y),
        (device_x, lax.rem(device_y + count_y // 2, count_y)),
    )
    sides = (device_x // (count_x // 2), device_y // (count_y // 2))
    starts = [sum(PIECES[:k]) for k in range(len(PIECES))]
    order = [(axis, at, width) for at, width in zip(starts, PIECES) for axis in (1, 0)]

    barrier = pltpu.get_barrier_semaphore()
    for partner in partners:
        pl.semaphore_signal(barrier, inc=1, device_id=partner, device_id_type=MESH)

    def load_block(j):
        axis, at, width = order[j]
        lanes = pl.ds(axis * half + at, width)
        return pltpu.make_async_copy(samples.at[:, :, lanes], x_ref.at[:, :, lanes], x_sem.at[j])

    def load_level(axis):
        return pltpu.make_async_copy(level_consts.at[axis, sides[axis]], levels.at[axis], level_sem)

    load_labels = pltpu.make_async_copy(labels_in, labels, label_sem)
    load_labels.start()
    load_block(0).start()
    for axis in range(2):
        load_level(axis).start()
    for j in range(1, len(order)):
        load_block(j).start()

    boxes_x = FB // FBY
    column = lax.broadcasted_iota(jnp.int32, (size_x, samples_box), 1)
    first_column = size_y * lax.broadcasted_iota(jnp.int32, (size_x, samples_box), 0)
    inside = (column >= first_column) & (column < first_column + size_y)
    spread[...] = jnp.where(inside, 1.0, 0.0).astype(jnp.bfloat16)
    row = lax.broadcasted_iota(jnp.int32, (boxes_x * Q1, 1), 0)
    centre = (row // Q1) * width_x + width_x // 2
    node = jnp.cos(jnp.pi * (2.0 * (row % Q1).astype(jnp.float32) + 1.0) / (2.0 * Q1))
    corner = ((device_x * size_x * centre) % N).astype(jnp.float32)
    step = lax.broadcasted_iota(jnp.int32, (boxes_x * Q1, size_x), 1).astype(jnp.float32)
    angle = 2.0 * jnp.pi * ((corner + (centre.astype(jnp.float32) + 0.5 * width_x * node) * step) / N)
    parts = jnp.concatenate([jnp.cos(angle), jnp.sin(angle)], axis=0)
    parts_high = parts.astype(jnp.bfloat16).astype(jnp.float32)
    for k, part in enumerate((parts_high, parts - parts_high)):
        repeated = jnp.dot(part.astype(jnp.bfloat16), spread[...], preferred_element_type=jnp.float32)
        repeated = repeated.reshape(2, boxes_x, Q1, samples_box)
        if k == 0:
            wide[...] = repeated
        else:
            wide[...] += repeated

    row = lax.broadcasted_iota(jnp.int32, (FBY * Q2, 1), 0)
    centre = (row // Q2) * width_y + width_y // 2
    node = jnp.cos(jnp.pi * (2.0 * (row % Q2).astype(jnp.float32) + 1.0) / (2.0 * Q2))
    corner = ((device_y * size_y * centre) % N).astype(jnp.float32)
    step = (lax.broadcasted_iota(jnp.int32, (FBY * Q2, 2 * size_y), 1) % size_y).astype(jnp.float32)
    angle = 2.0 * jnp.pi * ((corner + (centre.astype(jnp.float32) + 0.5 * width_y * node) * step) / N)
    narrow[0] = (jnp.cos(angle) + jnp.sin(angle)).reshape(FBY, Q2, 2 * size_y)
    narrow[1] = (jnp.cos(angle) - jnp.sin(angle)).reshape(FBY, Q2, 2 * size_y)
    load_labels.wait()

    def build_table(slot):
        label_x, label_y = labels[slot] // FBY, labels[slot] % FBY
        plus_y, minus_y = narrow[0, label_y], narrow[1, label_y]
        pair = 2 * size_y
        run = 4 * pair

        def fill(k, _):
            for i in range(Q1):
                for at in range(0, run, pair):
                    lanes = pl.ds(pl.multiple_of(k * run, run) + at, pair)
                    cos_x, sin_x = wide[0, label_x, i : i + 1, lanes], wide[1, label_x, i : i + 1, lanes]
                    table[i * Q2 : (i + 1) * Q2, lanes] = (cos_x * plus_y + sin_x * minus_y).astype(jnp.bfloat16)
            return 0

        lax.fori_loop(0, samples_box // run, fill, 0)

    whole = [(start, slots, 0, half) for start, slots in SENDS]
    pieces = [(0, 1, at, width) for at, width in zip(starts, PIECES)]
    sends = pieces + whole
    resends = [(start, slots, 0, half) for start, slots in RESENDS]

    def view(ref, axis, message):
        start, slots, at, width = message
        return ref.at[axis, pl.ds(start, slots), :, pl.ds(at, width)]

    def send(axis, k):
        return pltpu.make_async_remote_copy(
            src_ref=view(sent, axis, sends[k]), dst_ref=view(came, axis, sends[k]),
            send_sem=send_sem.at[axis], recv_sem=came_sem.at[axis, k],
            device_id=partners[axis], device_id_type=MESH,
        )

    def resend(axis, k):
        return pltpu.make_async_remote_copy(
            src_ref=view(came, axis, resends[k]), dst_ref=view(last, axis, resends[k]),
            send_sem=resend_sem.at[axis], recv_sem=last_sem.at[axis, k],
            device_id=partners[1 - axis], device_id_type=MESH,
        )

    def at_end(messages, slot, act, skip=0):
        for k, (start, slots, _, _) in enumerate(messages):
            if k >= skip:
                pl.when(slot == start + slots - 1)(functools.partial(act, k))

    def at_start(messages, slot, act):
        for k, (start, _, _, _) in enumerate(messages):
            pl.when(slot == start)(functools.partial(act, k))

    def first_level(axis, slot, at, width):
        lanes = slice(axis * half + at, axis * half + at + width)
        block = x_ref[:, :, lanes].reshape(samples_box, width)
        initial = norm * jnp.dot(table[...], block, preferred_element_type=jnp.float32)
        both = product(levels.at[axis], initial)
        total[slot, :, lanes] = both[:Q]
        sent[axis, slot, :, at : at + width] = both[Q:]

    build_table(0)
    for j, (axis, at, width) in enumerate(order):
        load_block(j).wait()
        if j == 0:
            pltpu.make_async_copy(level_consts.at[:, 0], levels, level_sem).wait()
        first_level(axis, 0, at, width)
        if j == 0:
            pl.semaphore_wait(barrier, 2)
        send(axis, starts.index(at)).start()

    def first(slot, _):
        build_table(slot)
        for axis in (1, 0):
            for at in range(0, half, LANES):
                first_level(axis, slot, at, LANES)
            at_end(sends, slot, lambda k, axis=axis: send(axis, k).start(), len(pieces))
        return 0

    lax.fori_loop(1, FB, first, 0)

    def second(slot, _):
        for axis in (1, 0):
            lanes = slice(axis * half, (axis + 1) * half)
            at_start(sends, slot, lambda k, axis=axis: send(axis, k).wait_recv())
            both = product(levels.at[1 - axis], total[slot, :, lanes] + came[axis, slot])
            total[slot, :, lanes] = both[:Q]
            came[axis, slot] = both[Q:]
            at_end(resends, slot, lambda k, axis=axis: resend(axis, k).start())
        return 0

    lax.fori_loop(0, FB, second, 0)

    def third(slot, _):
        for axis in (1, 0):
            lanes = slice(axis * half, (axis + 1) * half)
            at_start(resends, slot, lambda k, axis=axis: resend(axis, k).wait_recv())
            total[slot, :, lanes] += last[axis, slot]
        return 0

    lax.fori_loop(0, FB, third, 0)
    for axis in range(2):
        for source, target, out_sem, in_sem in ((sent, came, send_sem, came_sem), (came, last, resend_sem, last_sem)):
            pltpu.make_async_remote_copy(
                src_ref=source.at[axis], dst_ref=target.at[axis],
                send_sem=out_sem.at[axis], recv_sem=in_sem.at[axis, 0],
                device_id=partners[axis], device_id_type=MESH,
            ).wait_send()


def local(samples, box_labels):
    size_x, size_y, records = samples.shape
    ratio_x = 2.0 * size_x * (N // (2 * size_x)) / N
    ratio_y = 2.0 * size_y * (N // (2 * size_y)) / N
    consts = np.stack(
        [
            level_tables(Q1, ratio_x, lambda g: np.kron(g, np.eye(Q2))),
            level_tables(Q2, ratio_y, lambda g: np.kron(np.eye(Q1), g)),
        ]
    )
    half = records // 2
    held = pltpu.VMEM((2, FB, Q, half), jnp.float32)
    pair = pltpu.SemaphoreType.DMA((2,))
    total = pl.pallas_call(
        kernel,
        in_specs=[
            pl.BlockSpec(memory_space=pl.ANY),
            pl.BlockSpec(memory_space=pl.ANY),
            pl.BlockSpec(memory_space=pl.ANY),
        ],
        out_specs=pl.BlockSpec(memory_space=pltpu.VMEM),
        out_shape=pltpu.VMEM((FB, Q, records), jnp.float32),
        scratch_shapes=[
            pltpu.SMEM(box_labels.shape, jnp.int32),
            pltpu.VMEM(samples.shape, jnp.bfloat16),
            pltpu.VMEM((2, 2, 2 * Q, Q), jnp.bfloat16),
            pltpu.VMEM((size_x, size_x * size_y), jnp.bfloat16),
            pltpu.VMEM((2, FB // FBY, Q1, size_x * size_y), jnp.float32),
            pltpu.VMEM((2, FBY, Q2, 2 * size_y), jnp.float32),
            pltpu.VMEM((Q, size_x * size_y), jnp.bfloat16),
            held, held, held,
            pltpu.SemaphoreType.DMA,
            pltpu.SemaphoreType.DMA((2 * len(PIECES),)),
            pltpu.SemaphoreType.DMA,
            pair, pltpu.SemaphoreType.DMA((2, len(PIECES) + len(SENDS))),
            pair, pltpu.SemaphoreType.DMA((2, len(RESENDS))),
        ],
        compiler_params=pltpu.CompilerParams(collective_id=0, has_side_effects=True, vmem_limit_bytes=46 << 20),
    )(box_labels, samples, jnp.asarray(consts))
    return total.reshape(1, 1, FB * Q, records)


def solution(mesh):
    in_specs = (P("gx", "gy", None), P())
    out_specs = P("gx", "gy", None, None)
    return jax.shard_map(local, mesh=mesh, in_specs=in_specs, out_specs=out_specs, check_vma=False)
```

```python
import functools
import math

import jax
import jax.numpy as jnp
import numpy as np
from jax import lax
from jax.experimental import pallas as pl
from jax.experimental.pallas import tpu as pltpu
from jax.sharding import PartitionSpec as P

N = 16384
FBY = 4
FB = 16
Q1 = 8
Q2 = 16
Q = Q1 * Q2
LANES = 512
PIECES = (128, 128, 256)
MESH = pl.DeviceIdType.MESH
SENDS = ((1, 1), (2, 2), (4, 4), (8, 8))
RESENDS = ((0, 4), (4, 8), (12, 3), (15, 1))


def cheb_nodes(points):
    return np.cos(np.pi * (2.0 * np.arange(points) + 1.0) / (2.0 * points))


def level_matrix(points, box_ratio, side, child):
    nodes = cheb_nodes(points)
    targets = child - 0.5 + 0.5 * nodes
    weights = np.ones((points, points))
    for m in range(points):
        for other in range(points):
            if other != m:
                weights[:, m] *= (targets - nodes[other]) / (nodes[m] - nodes[other])
    turns = ((child - 0.5) * 0.5 + 0.25 * nodes[:, None] - 0.5 * nodes[None, :]) * (box_ratio * (side - 0.5) * 0.5)
    radians = 2.0 * np.pi * turns
    return weights * (np.cos(radians) + np.sin(radians))


def level_tables(points, box_ratio, spread):
    both = np.stack(
        [
            np.concatenate([spread(level_matrix(points, box_ratio, s, c)) for c in (s, 1 - s)], axis=0)
            for s in (0, 1)
        ]
    ).astype(np.float32)
    high = both.astype(jnp.bfloat16)
    low = (both - high.astype(np.float32)).astype(jnp.bfloat16)
    return np.stack([high, low], axis=1)


def product(tables, value):
    high, low = tables[0], tables[1]
    value_high = value.astype(jnp.bfloat16)
    value_low = (value - value_high.astype(jnp.float32)).astype(jnp.bfloat16)
    dot = functools.partial(jnp.dot, preferred_element_type=jnp.float32)
    return dot(high, value_high) + (dot(low, value_high) + dot(high, value_low))


def kernel(
    labels_in, samples, level_consts, total,
    labels, x_ref, levels, spread, wide, narrow, table, sent, came, last,
    label_sem, x_sem, level_sem, send_sem, came_sem, resend_sem, last_sem,
):
    size_x, size_y, records = samples.shape
    samples_box = size_x * size_y
    width_x, width_y = N // (2 * size_x), N // (2 * size_y)
    norm = 1.0 / math.sqrt(samples_box)
    half = records // 2
    count_x, count_y = lax.axis_size("gx"), lax.axis_size("gy")
    device_x, device_y = lax.axis_index("gx"), lax.axis_index("gy")
    partners = (
        (lax.rem(device_x + count_x // 2, count_x), device_y),
        (device_x, lax.rem(device_y + count_y // 2, count_y)),
    )
    sides = (device_x // (count_x // 2), device_y // (count_y // 2))
    starts = [sum(PIECES[:k]) for k in range(len(PIECES))]
    order = [(axis, at, width) for at, width in zip(starts, PIECES) for axis in (1, 0)]

    barrier = pltpu.get_barrier_semaphore()
    for partner in partners:
        pl.semaphore_signal(barrier, inc=1, device_id=partner, device_id_type=MESH)

    def load_block(j):
        axis, at, width = order[j]
        lanes = pl.ds(axis * half + at, width)
        return pltpu.make_async_copy(samples.at[:, :, lanes], x_ref.at[:, :, lanes], x_sem.at[j])

    def load_level(axis):
        return pltpu.make_async_copy(level_consts.at[axis, sides[axis]], levels.at[axis], level_sem)

    load_labels = pltpu.make_async_copy(labels_in, labels, label_sem)
    load_labels.start()
    load_block(0).start()
    for axis in range(2):
        load_level(axis).start()
    for j in range(1, len(order)):
        load_block(j).start()

    boxes_x = FB // FBY
    column = lax.broadcasted_iota(jnp.int32, (size_x, samples_box), 1)
    first_column = size_y * lax.broadcasted_iota(jnp.int32, (size_x, samples_box), 0)
    inside = (column >= first_column) & (column < first_column + size_y)
    spread[...] = jnp.where(inside, 1.0, 0.0).astype(jnp.bfloat16)
    row = lax.broadcasted_iota(jnp.int32, (boxes_x * Q1, 1), 0)
    centre = (row // Q1) * width_x + width_x // 2
    node = jnp.cos(jnp.pi * (2.0 * (row % Q1).astype(jnp.float32) + 1.0) / (2.0 * Q1))
    corner = ((device_x * size_x * centre) % N).astype(jnp.float32)
    step = lax.broadcasted_iota(jnp.int32, (boxes_x * Q1, size_x), 1).astype(jnp.float32)
    angle = 2.0 * jnp.pi * ((corner + (centre.astype(jnp.float32) + 0.5 * width_x * node) * step) / N)
    parts = jnp.concatenate([jnp.cos(angle), jnp.sin(angle)], axis=0)
    parts_high = parts.astype(jnp.bfloat16).astype(jnp.float32)
    for k, part in enumerate((parts_high, parts - parts_high)):
        repeated = jnp.dot(part.astype(jnp.bfloat16), spread[...], preferred_element_type=jnp.float32)
        repeated = repeated.reshape(2, boxes_x, Q1, samples_box)
        if k == 0:
            wide[...] = repeated
        else:
            wide[...] += repeated

    row = lax.broadcasted_iota(jnp.int32, (FBY * Q2, 1), 0)
    centre = (row // Q2) * width_y + width_y // 2
    node = jnp.cos(jnp.pi * (2.0 * (row % Q2).astype(jnp.float32) + 1.0) / (2.0 * Q2))
    corner = ((device_y * size_y * centre) % N).astype(jnp.float32)
    step = (lax.broadcasted_iota(jnp.int32, (FBY * Q2, 2 * size_y), 1) % size_y).astype(jnp.float32)
    angle = 2.0 * jnp.pi * ((corner + (centre.astype(jnp.float32) + 0.5 * width_y * node) * step) / N)
    narrow[0] = (jnp.cos(angle) + jnp.sin(angle)).reshape(FBY, Q2, 2 * size_y)
    narrow[1] = (jnp.cos(angle) - jnp.sin(angle)).reshape(FBY, Q2, 2 * size_y)
    load_labels.wait()

    def build_table(slot):
        label_x, label_y = labels[slot] // FBY, labels[slot] % FBY
        plus_y, minus_y = narrow[0, label_y], narrow[1, label_y]
        pair = 2 * size_y
        run = 4 * pair

        def fill(k, _):
            for i in range(Q1):
                for at in range(0, run, pair):
                    lanes = pl.ds(pl.multiple_of(k * run, run) + at, pair)
                    cos_x, sin_x = wide[0, label_x, i : i + 1, lanes], wide[1, label_x, i : i + 1, lanes]
                    table[i * Q2 : (i + 1) * Q2, lanes] = (cos_x * plus_y + sin_x * minus_y).astype(jnp.bfloat16)
            return 0

        lax.fori_loop(0, samples_box // run, fill, 0)

    whole = [(start, slots, 0, half) for start, slots in SENDS]
    pieces = [(0, 1, at, width) for at, width in zip(starts, PIECES)]
    sends = pieces + whole
    resends = [(start, slots, 0, half) for start, slots in RESENDS]

    def view(ref, axis, message):
        start, slots, at, width = message
        return ref.at[axis, pl.ds(start, slots), :, pl.ds(at, width)]

    def send(axis, k):
        return pltpu.make_async_remote_copy(
            src_ref=view(sent, axis, sends[k]), dst_ref=view(came, axis, sends[k]),
            send_sem=send_sem.at[axis], recv_sem=came_sem.at[axis, k],
            device_id=partners[axis], device_id_type=MESH,
        )

    def resend(axis, k):
        return pltpu.make_async_remote_copy(
            src_ref=view(came, axis, resends[k]), dst_ref=view(last, axis, resends[k]),
            send_sem=resend_sem.at[axis], recv_sem=last_sem.at[axis, k],
            device_id=partners[1 - axis], device_id_type=MESH,
        )

    def at_end(messages, slot, act, skip=0):
        for k, (start, slots, _, _) in enumerate(messages):
            if k >= skip:
                pl.when(slot == start + slots - 1)(functools.partial(act, k))

    def at_start(messages, slot, act):
        for k, (start, _, _, _) in enumerate(messages):
            pl.when(slot == start)(functools.partial(act, k))

    def first_level(axis, slot, at, width):
        lanes = slice(axis * half + at, axis * half + at + width)
        block = x_ref[:, :, lanes].reshape(samples_box, width)
        initial = norm * jnp.dot(table[...], block, preferred_element_type=jnp.float32)
        both = product(levels.at[axis], initial)
        total[slot, :, lanes] = both[:Q]
        sent[axis, slot, :, at : at + width] = both[Q:]

    build_table(0)
    for j, (axis, at, width) in enumerate(order):
        load_block(j).wait()
        if j == 0:
            pltpu.make_async_copy(level_consts.at[:, 0], levels, level_sem).wait()
        first_level(axis, 0, at, width)
        if j == 0:
            pl.semaphore_wait(barrier, 2)
        send(axis, starts.index(at)).start()

    def first(slot, _):
        build_table(slot)
        for axis in (1, 0):
            for at in range(0, half, LANES):
                first_level(axis, slot, at, LANES)
            at_end(sends, slot, lambda k, axis=axis: send(axis, k).start(), len(pieces))
        return 0

    lax.fori_loop(1, FB, first, 0)

    def second(slot, _):
        for axis in (1, 0):
            lanes = slice(axis * half, (axis + 1) * half)
            at_start(sends, slot, lambda k, axis=axis: send(axis, k).wait_recv())
            both = product(levels.at[1 - axis], total[slot, :, lanes] + came[axis, slot])
            total[slot, :, lanes] = both[:Q]
            came[axis, slot] = both[Q:]
            at_end(resends, slot, lambda k, axis=axis: resend(axis, k).start())
        return 0

    lax.fori_loop(0, FB, second, 0)

    def third(slot, _):
        for axis in (1, 0):
            lanes = slice(axis * half, (axis + 1) * half)
            at_start(resends, slot, lambda k, axis=axis: resend(axis, k).wait_recv())
            total[slot, :, lanes] += last[axis, slot]
        return 0

    lax.fori_loop(0, FB, third, 0)
    for axis in range(2):
        for source, target, out_sem, in_sem in ((sent, came, send_sem, came_sem), (came, last, resend_sem, last_sem)):
            pltpu.make_async_remote_copy(
                src_ref=source.at[axis], dst_ref=target.at[axis],
                send_sem=out_sem.at[axis], recv_sem=in_sem.at[axis, 0],
                device_id=partners[axis], device_id_type=MESH,
            ).wait_send()


def local(samples, box_labels):
    size_x, size_y, records = samples.shape
    ratio_x = 2.0 * size_x * (N // (2 * size_x)) / N
    ratio_y = 2.0 * size_y * (N // (2 * size_y)) / N
    consts = np.stack(
        [
            level_tables(Q1, ratio_x, lambda g: np.kron(g, np.eye(Q2))),
            level_tables(Q2, ratio_y, lambda g: np.kron(np.eye(Q1), g)),
        ]
    )
    half = records // 2
    held = pltpu.VMEM((2, FB, Q, half), jnp.float32)
    pair = pltpu.SemaphoreType.DMA((2,))
    total = pl.pallas_call(
        kernel,
        in_specs=[
            pl.BlockSpec(memory_space=pl.ANY),
            pl.BlockSpec(memory_space=pl.ANY),
            pl.BlockSpec(memory_space=pl.ANY),
        ],
        out_specs=pl.BlockSpec(memory_space=pltpu.VMEM),
        out_shape=pltpu.VMEM((FB, Q, records), jnp.float32),
        scratch_shapes=[
            pltpu.SMEM(box_labels.shape, jnp.int32),
            pltpu.VMEM(samples.shape, jnp.bfloat16),
            pltpu.VMEM((2, 2, 2 * Q, Q), jnp.bfloat16),
            pltpu.VMEM((size_x, size_x * size_y), jnp.bfloat16),
            pltpu.VMEM((2, FB // FBY, Q1, size_x * size_y), jnp.float32),
            pltpu.VMEM((2, FBY, Q2, 2 * size_y), jnp.float32),
            pltpu.VMEM((Q, size_x * size_y), jnp.bfloat16),
            held, held, held,
            pltpu.SemaphoreType.DMA,
            pltpu.SemaphoreType.DMA((2 * len(PIECES),)),
            pltpu.SemaphoreType.DMA,
            pair, pltpu.SemaphoreType.DMA((2, len(PIECES) + len(SENDS))),
            pair, pltpu.SemaphoreType.DMA((2, len(RESENDS))),
        ],
        compiler_params=pltpu.CompilerParams(collective_id=0, has_side_effects=True, vmem_limit_bytes=46 << 20),
    )(box_labels, samples, jnp.asarray(consts))
    return total.reshape(1, 1, FB * Q, records)


def solution(mesh):
    in_specs = (P("gx", "gy", None), P())
    out_specs = P("gx", "gy", None, None)
    return jax.shard_map(local, mesh=mesh, in_specs=in_specs, out_specs=out_specs, check_vma=False)
```
